32 devices in a mesh: group: 2 (over y), slab: 4 (over z), shot: 4 (over x, core).
Axes of the slice: x: 2, y: 2, z: 4, core: 2. Of those that a mesh axis runs over, the one named last changes fastest.
Arguments:
- source_state: float32 [32, 5, 32, 512], P(('group', 'shot'), None, 'slab'), parts along dimension 0, may hold values from -6 to 6
- receiver_state: float32 [32, 5, 32, 512], P(('group', 'shot'), None, 'slab'), parts along dimension 0, may hold values from -6 to 6
- p_velocity: float32 [64, 512], P(('group', 'slab')), parts along dimension 0, may hold values from 1 to 2
- s_velocity: float32 [64, 512], P(('group', 'slab')), parts along dimension 0, may hold values from 0.4 to 0.65
- density: float32 [64, 512], P(('group', 'slab')), parts along dimension 0, may hold values from 1 to 2
- receiver_data: float32 [32, 4, 256], P(('group', 'shot')), parts along dimension 0, may hold values from -6 to 6
- source_x: int32 [32], P(('group', 'shot')), parts along dimension 0, may hold values from 0 to 31
- source_z: int32 [32], P(('group', 'shot')), parts along dimension 0, may hold values from 0 to 511
- receiver_x: int32 [512], P('group'), parts along dimension 0, may hold values from 0 to 31
- receiver_z: int32 [512], P('group'), parts along dimension 0, may hold values from 0 to 511
- offsets: int32 [64], replicated, may hold values from -32 to 32, as said below
Outputs:
- final_source: float32 [32, 5, 32, 512], P(('group', 'shot'), None, 'slab'), parts along dimension 0
- final_receiver: float32 [32, 5, 32, 512], P(('group', 'shot'), None, 'slab'), parts along dimension 0
- vp_image: float32 [128, 32, 512], P(('group', 'shot'), 'slab'), parts along dimension 0
- vs_image: float32 [128, 32, 512], P(('group', 'shot'), 'slab'), parts along dimension 0
- rho_image: float32 [128, 32, 512], P(('group', 'shot'), 'slab'), parts along dimension 0
The draws below stay inside these ranges and needn't reach their ends.
There are 2 independent parts, one for each index of `group`. The reference program is written for one: setup_inputs(seed, part) draws one part's arguments, and reference() takes and returns one part's arrays. A program takes and returns all parts, laid end to end along the dimension named above; an argument that names none is the same for every part. Nothing has to cross between parts.
Inputs may be any that keep to these rules, and one draw needn't show every extreme that they name: 64 distinct offsets in increasing order; -32 and 32 are among them.
All inputs are finite; a program needn't handle non-finite values.
Results may differ from the reference program's by a relative error of at most 0.0032.
Values may be sent and summed in bfloat16 or wider, within the bound.
A program may use at most 64 MiB of HBM per device.

```python
import math
import jax
import jax.numpy as jnp
from jax import lax

NZ = 512
STEPS = 4
NOFF = 64
SHIFT = 32
NREC = 256
NX = 32
SHOTS = 16


def draw_offsets(key, part):
    key = jax.random.fold_in(key, 11)
    inner = jax.random.permutation(key, 2 * SHIFT - 1)[:NOFF - 2].astype(jnp.int32) - (SHIFT - 1)
    ends = jnp.array([-SHIFT, SHIFT], jnp.int32)
    return jnp.sort(jnp.concatenate([ends, inner]))


def with_ends(values, own_key, smallest, high):
    shape = values.shape
    spot = [jax.random.randint(jax.random.fold_in(own_key, axis), (), 0, shape[axis]) for axis in range(len(shape))]
    values = values.at[tuple(spot)].set(smallest)
    longest = shape.index(max(shape))
    spot[longest] = (spot[longest] + 1) % shape[longest]
    return values.at[tuple(spot)].set(high)


def block_scale(key, dims, shards, smallest, top_value):
    def one(position, blocks):
        heights = jax.random.uniform(jax.random.fold_in(jax.random.fold_in(key, 6), position), (blocks,), jnp.float32, smallest / len(shards), top_value / len(shards))
        return jnp.repeat(jnp.exp(heights), dims[position] // blocks).reshape((-1,) + (1,) * (len(dims) - position - 1))

    factor_of = one(*shards[0])
    for cut in shards[1:]:
        factor_of = factor_of * one(*cut)
    return factor_of


def normal_values(own_key, extent, scale, most, pieces=(), dtype=jnp.bfloat16):
    result = jax.random.normal(own_key, extent, jnp.float32) * scale
    if len(pieces) > 0:
        result = block_scale(own_key, extent, pieces, -0.22, 0.18) * result
    return jnp.clip(result, min=-most, max=most).astype(dtype)


def setup_inputs(seed: int = 0, part: int = 0) -> dict:
    keys = jax.random.split(jax.random.key(seed), 12)
    own_keys = jax.random.split(jax.random.fold_in(keys[11], part), 12)
    source_state = normal_values(own_keys[0], (SHOTS, 5, NX, NZ), 1.0, 6.0, ((0, 4), (2, 4)), jnp.float32)
    receiver_state = normal_values(own_keys[1], (SHOTS, 5, NX, NZ), 1.0, 6.0, ((0, 4), (2, 4)), jnp.float32)
    p_velocity = jnp.clip(1.0 + 1.0 * jax.random.uniform(own_keys[2], (NX, NZ), jnp.float32) ** block_scale(own_keys[2], (NX, NZ), ((0, 4),), -0.2, 0.2), 1.0, 2.0)
    s_velocity = jnp.clip(0.4 + 0.24999997 * jax.random.uniform(own_keys[3], (NX, NZ), jnp.float32) ** block_scale(own_keys[3], (NX, NZ), ((0, 4),), -0.2, 0.2), 0.4, 0.65)
    density = jnp.clip(1.0 + 1.0 * jax.random.uniform(own_keys[4], (NX, NZ), jnp.float32) ** block_scale(own_keys[4], (NX, NZ), ((0, 4),), -0.2, 0.2), 1.0, 2.0)
    receiver_data = normal_values(own_keys[5], (SHOTS, STEPS, NREC), 1.0, 6.0, ((0, 4),), jnp.float32)
    source_x = with_ends(jax.random.randint(own_keys[6], (SHOTS,), 0, NX), jax.random.fold_in(own_keys[6], 1), 0, NX - 1).astype(jnp.int32)
    source_z = with_ends(jax.random.randint(own_keys[7], (SHOTS,), 0, NZ), jax.random.fold_in(own_keys[7], 1), 0, NZ - 1).astype(jnp.int32)
    receiver_x = with_ends(jax.random.randint(own_keys[8], (NREC,), 0, NX), jax.random.fold_in(own_keys[8], 1), 0, NX - 1).astype(jnp.int32)
    receiver_z = with_ends(jax.random.randint(own_keys[9], (NREC,), 0, NZ), jax.random.fold_in(own_keys[9], 1), 0, NZ - 1).astype(jnp.int32)
    offsets = draw_offsets(jax.random.fold_in(keys[11], 71), part)
    return dict(source_state=source_state, receiver_state=receiver_state, p_velocity=p_velocity, s_velocity=s_velocity, density=density, receiver_data=receiver_data, source_x=source_x, source_z=source_z, receiver_x=receiver_x, receiver_z=receiver_z, offsets=offsets)


time_step = 0.3


def back_x(field):
    return field - jnp.pad(field, ((0, 0), (0, 0), (1, 0), (0, 0)))[:, :, :-1, :]


def fore_x(field):
    return jnp.pad(field, ((0, 0), (0, 0), (0, 1), (0, 0)))[:, :, 1:, :] - field


def back_z(field):
    return field - jnp.pad(field, ((0, 0), (0, 0), (0, 0), (1, 0)))[:, :, :, :-1]


def fore_z(field):
    return jnp.pad(field, ((0, 0), (0, 0), (0, 0), (0, 1)))[:, :, :, 1:] - field


def reference(source_state, receiver_state, p_velocity, s_velocity, density, receiver_data, source_x, source_z, receiver_x, receiver_z, offsets):
    fields = [jnp.stack([source_state[:, index], receiver_state[:, index]]) for index in range(5)]
    velocity_x, velocity_z, stress_xx, stress_zz, stress_xz = fields
    buoyancy = 1.0 / density
    shear = density * s_velocity * s_velocity
    lame_first = density * (p_velocity * p_velocity - 2.0 * s_velocity * s_velocity)
    modulus = lame_first + 2.0 * shear
    signs = jnp.array([time_step, -time_step], jnp.float32).reshape(2, 1, 1, 1)
    shot_index = jnp.arange(SHOTS)
    source_list, pressure_list, rotation_list = [], [], []
    for step_index in range(STEPS):
        velocity_x = velocity_x + signs * buoyancy * (back_x(stress_xx) + back_z(stress_xz))
        velocity_z = velocity_z + signs * buoyancy * (fore_x(stress_xz) + fore_z(stress_zz))
        stretch = fore_x(velocity_x)
        squeeze = back_z(velocity_z)
        slide_x = back_x(velocity_z)
        slide_z = fore_z(velocity_x)
        stress_xx = stress_xx + signs * (modulus * stretch + lame_first * squeeze)
        stress_zz = stress_zz + signs * (lame_first * stretch + modulus * squeeze)
        stress_xz = stress_xz + signs * shear * (slide_x + slide_z)
        rotation = slide_z[1] - slide_x[1]
        wavelet = 2.0 * math.cos(1.3 * step_index + 0.4)
        source_add = jnp.zeros((SHOTS, NX, NZ), jnp.float32).at[shot_index, source_x, source_z].add(jnp.full((SHOTS,), wavelet, jnp.float32))
        receiver_add = jnp.zeros((SHOTS, NX, NZ), jnp.float32).at[:, receiver_x, receiver_z].add(receiver_data[:, step_index, :])
        inject = jnp.stack([source_add, receiver_add])
        stress_xx = stress_xx + inject
        stress_zz = stress_zz + inject
        pressure = (-0.5 * (stress_xx + stress_zz)).astype(jnp.bfloat16)
        source_list.append(pressure[0])
        pressure_list.append(pressure[1])
        rotation_list.append(rotation.astype(jnp.bfloat16))
    source_p = jnp.stack(source_list).astype(jnp.float32)
    padding = ((0, 0), (0, 0), (SHIFT, SHIFT), (0, 0))
    padded_p = jnp.pad(jnp.stack(pressure_list).astype(jnp.float32), padding)
    padded_s = jnp.pad(jnp.stack(rotation_list).astype(jnp.float32), padding)
    scale = 1.0 / (SHOTS * STEPS)

    def one_offset(offset):
        start = (offset + SHIFT).astype(jnp.int32)
        moved_p = lax.dynamic_slice_in_dim(padded_p, start, NX, 2)
        moved_s = lax.dynamic_slice_in_dim(padded_s, start, NX, 2)
        image_pp = jnp.sum(source_p * moved_p, axis=(0, 1))
        image_ps = jnp.sum(source_p * moved_s, axis=(0, 1))
        return jnp.stack([image_pp, image_ps]) * scale

    images = lax.map(one_offset, offsets)
    image_pp = images[:, 0]
    image_ps = images[:, 1]
    ratio = s_velocity / p_velocity
    vp_image = 2.0 * density * p_velocity * image_pp
    vs_image = 2.0 * density * s_velocity * (image_ps - 2.0 * ratio * ratio * image_pp)
    rho_image = p_velocity * p_velocity * image_pp + s_velocity * s_velocity * image_ps
    final_fields = (velocity_x, velocity_z, stress_xx, stress_zz, stress_xz)
    final_source = jnp.stack([field[0] for field in final_fields], axis=1)
    final_receiver = jnp.stack([field[1] for field in final_fields], axis=1)
    return (final_source, final_receiver, vp_image, vs_image, rho_image)
```

```python
import functools
import math

import jax
import jax.numpy as jnp
from jax import lax
from jax.experimental import pallas as pl
from jax.experimental.pallas import tpu as pltpu
from jax.sharding import PartitionSpec as P

STEPS = 4
SHIFT = 32
LANES = 128
DT = 0.3
F32 = jnp.float32
BF16 = jnp.bfloat16
MESH = pl.DeviceIdType.MESH


def kernel(
    n_slab, n_shot, reach, shots, noff,
    src_ref, rec_ref, vp_ref, vs_ref, rho_ref, data_ref, sx_ref, sz_ref, rx_ref, rz_ref, off_ref,
    fs_ref, fr_ref, ovp_ref, ovs_ref, orho_ref,
    model, inj, spread, rho_l, rho_r, to_r, to_l, from_l, from_r, edge, srcf, win, wf,
    part, part_bf, r1, s2, r2,
    halo_send, halo_recv, rho_send, rho_recv, win_send, win_recv, r1_send, r1_recv, r2_send, r2_recv,
):
    width, depth = rho_ref.shape
    zc_n = depth // LANES
    per = noff // n_shot
    na = n_shot // 2
    span = SHIFT // width
    me = lax.axis_index("slab")
    shot = lax.axis_index("shot")
    par = lax.rem(shot, 2)
    mate = shot + 1 - 2 * par
    mine = shot // 2
    has_l = me > 0
    has_r = me < n_slab - 1

    barrier = pltpu.get_barrier_semaphore()

    def greet(axis, index):
        pl.semaphore_signal(barrier, inc=1, device_id={axis: index}, device_id_type=MESH)

    for k in range(1, reach + 1):
        pl.when(me - k >= 0)(functools.partial(greet, "slab", me - k))
        pl.when(me + k < n_slab)(functools.partial(greet, "slab", me + k))
    greet("shot", mate)
    for q in range(1, na):
        greet("shot", 2 * lax.rem(mine + q, na) + par)

    row = lax.broadcasted_iota(jnp.int32, (width, depth), 0)
    lane = lax.broadcasted_iota(jnp.int32, (width, depth), 1)

    def back_z(f):
        return f - jnp.where(lane == 0, 0.0, pltpu.roll(f, 1, 1))

    def fore_z(f):
        return jnp.where(lane == depth - 1, 0.0, pltpu.roll(f, depth - 1, 1)) - f

    def down(f, halo):
        return jnp.where(row == 0, halo, pltpu.roll(f, 1, 0))

    def up(f, halo):
        return jnp.where(row == width - 1, halo, pltpu.roll(f, width - 1, 0))

    def pack(t, ws, fields):
        vx, vz, sxx, szz, sxz = fields
        one = pl.ds(ws, 1)
        for slot, f in enumerate((sxx, szz, sxz, vz)):
            to_r[t, slot, one, :] = f[width - 1 : width, :]
        for slot, f in enumerate((vx, sxx, sxz)):
            to_l[t, slot, one, :] = f[0:1, :]

    for w, ref in enumerate((src_ref, rec_ref)):

        def first(s, carry, w=w, ref=ref):
            pack(0, w * shots + s, [ref[s, i] for i in range(5)])
            return carry

        lax.fori_loop(0, shots, first, 0)

    count = sum(
        (me - k >= 0).astype(jnp.int32) + (me + k < n_slab).astype(jnp.int32)
        for k in range(1, reach + 1)
    ) + na
    pl.semaphore_wait(barrier, count)

    def halo_copy(t, right):
        if right:
            return pltpu.make_async_remote_copy(
                src_ref=to_r.at[t], dst_ref=from_l.at[t],
                send_sem=halo_send.at[t, 0], recv_sem=halo_recv.at[t, 0],
                device_id={"slab": me + 1}, device_id_type=MESH)
        return pltpu.make_async_remote_copy(
            src_ref=to_l.at[t], dst_ref=from_r.at[t],
            send_sem=halo_send.at[t, 1], recv_sem=halo_recv.at[t, 1],
            device_id={"slab": me - 1}, device_id_type=MESH)

    def rho_copy(right):
        if right:
            return pltpu.make_async_remote_copy(
                src_ref=rho_ref, dst_ref=rho_l, send_sem=rho_send.at[0], recv_sem=rho_recv.at[0],
                device_id={"slab": me + 1}, device_id_type=MESH)
        return pltpu.make_async_remote_copy(
            src_ref=rho_ref, dst_ref=rho_r, send_sem=rho_send.at[1], recv_sem=rho_recv.at[1],
            device_id={"slab": me - 1}, device_id_type=MESH)

    def send_halo(t):
        pl.when(has_r)(lambda: halo_copy(t, True).start())
        pl.when(has_l)(lambda: halo_copy(t, False).start())

    send_halo(0)
    pl.when(has_r)(lambda: rho_copy(True).start())
    pl.when(has_l)(lambda: rho_copy(False).start())

    def win_copy(t, from_slot, to_slot, target):
        return pltpu.make_async_remote_copy(
            src_ref=win.at[t, from_slot], dst_ref=win.at[t, to_slot],
            send_sem=win_send.at[t, to_slot], recv_sem=win_recv.at[t, to_slot],
            device_id={"slab": target}, device_id_type=MESH)

    def hop(t, k):
        right = win_copy(t, reach - k + 1, reach - k, me + 1)
        left = win_copy(t, reach + k - 1, reach + k, me - 1)
        pl.when(has_r & (me - k + 1 >= 0))(lambda: right.start())
        pl.when(has_l & (me + k - 1 < n_slab))(lambda: left.start())

    def hop_wait(t, k):
        pl.when(me - k >= 0)(lambda: win_copy(t, reach - k + 1, reach - k, me + 1).wait_recv())
        pl.when(me + k < n_slab)(lambda: win_copy(t, reach + k - 1, reach + k, me - 1).wait_recv())

    def hop_done(t, k):
        pl.when(has_r & (me - k + 1 >= 0))(
            lambda: win_copy(t, reach - k + 1, reach - k, me + 1).wait_send())
        pl.when(has_l & (me + k - 1 < n_slab))(
            lambda: win_copy(t, reach + k - 1, reach + k, me - 1).wait_send())

    rho = rho_ref[...]
    vp = vp_ref[...]
    vs = vs_ref[...]
    shear = rho * vs * vs
    lame = rho * (vp * vp - 2.0 * vs * vs)
    model[0] = 1.0 / rho
    model[1] = shear
    model[2] = lame
    model[3] = lame + 2.0 * shear

    @pl.when(jnp.logical_not(has_l))
    def _():
        from_l[...] = jnp.zeros_like(from_l)
        rho_l[...] = jnp.ones_like(rho_l)

    @pl.when(jnp.logical_not(has_r))
    def _():
        from_r[...] = jnp.zeros_like(from_r)
        rho_r[...] = jnp.ones_like(rho_r)

    nrec = data_ref.shape[2]
    rel = rx_ref[...] - me * width
    at_x = rel == lax.broadcasted_iota(jnp.int32, (width, nrec), 0)
    for s in range(shots):
        for t in range(STEPS):
            spread[pl.ds((t * shots + s) * width, width), :] = jnp.where(
                at_x, data_ref[s, t : t + 1, :], 0.0)
    at_z = jnp.where(
        lax.broadcasted_iota(jnp.int32, (depth, nrec), 0) == rz_ref[...], 1.0, 0.0).astype(BF16)
    rest = spread[...]
    total = None
    for _ in range(3):
        piece = rest.astype(BF16)
        rest = rest - piece.astype(F32)
        term = lax.dot_general(piece, at_z, (((1,), (1,)), ((), ())), preferred_element_type=F32)
        total = term if total is None else total + term
    inj[...] = total

    def zero(i, carry):
        wf[0, i] = jnp.zeros(wf.shape[2:], F32)
        wf[1, i] = jnp.zeros(wf.shape[2:], F32)
        return carry

    lax.fori_loop(0, STEPS * shots, zero, 0)

    sign_rows = jnp.where(row < shots, DT, -DT)

    def widen(t, slot):
        base = (slot - reach + span) * width

        def body(s, carry):
            both = win[t, slot, s].astype(F32)
            for zc in range(zc_n):
                cut = both[:, zc * LANES : (zc + 1) * LANES]
                wf[0, t * shots + s, zc, base : base + width, :] = cut[:width]
                wf[1, t * shots + s, zc, base : base + width, :] = cut[width:]
            return carry

        lax.fori_loop(0, shots, body, 0)

    for t in range(STEPS):
        pl.when(has_l)(lambda: halo_copy(t, True).wait_recv())
        pl.when(has_r)(lambda: halo_copy(t, False).wait_recv())
        if t == 0:
            pl.when(has_l)(lambda: rho_copy(True).wait_recv())
            pl.when(has_r)(lambda: rho_copy(False).wait_recv())
        buoy_l = jnp.where(has_l, 1.0 / rho_l[width - 1 : width, :], 0.0)
        buoy_r = jnp.where(has_r, 1.0 / rho_r[0:1, :], 0.0)
        edge[0] = from_l[t, 3] + sign_rows * buoy_l * (
            to_l[t, 2] - from_l[t, 2] + fore_z(from_l[t, 1]))
        edge[1] = from_r[t, 0] + sign_rows * buoy_r * (
            from_r[t, 1] - to_r[t, 0] + back_z(from_r[t, 2]))
        wavelet = 2.0 * math.cos(1.3 * t + 0.4)
        for w in range(2):
            state = (fs_ref, fr_ref)[w]
            before = ((src_ref, rec_ref)[w]) if t == 0 else state
            sg = (DT, -DT)[w]

            def step(s, carry, w=w, state=state, before=before, sg=sg, t=t, wavelet=wavelet):
                ws = w * shots + s
                one = pl.ds(ws, 1)
                vx, vz, sxx, szz, sxz = [before[s, i] for i in range(5)]
                buoy = sg * model[0]
                vx = vx + buoy * (sxx - down(sxx, from_l[t, 0, one, :]) + back_z(sxz))
                vz = vz + buoy * (up(sxz, from_r[t, 2, one, :]) - sxz + fore_z(szz))
                stretch = sg * (up(vx, edge[1, one, :]) - vx)
                squeeze = sg * back_z(vz)
                slide_x = vz - down(vz, edge[0, one, :])
                slide_z = fore_z(vx)
                if w == 0:
                    here = (row + me * width == sx_ref[s]) & (lane == sz_ref[s])
                    add = jnp.where(here, wavelet, 0.0)
                else:
                    start = pl.multiple_of((t * shots + s) * width, width)
                    add = inj[pl.ds(start, width), :]
                sxx = sxx + (model[3] * stretch + model[2] * squeeze) + add
                szz = szz + (model[2] * stretch + model[3] * squeeze) + add
                sxz = sxz + sg * model[1] * (slide_x + slide_z)
                for i, f in enumerate((vx, vz, sxx, szz, sxz)):
                    state[s, i] = f
                if t < STEPS - 1:
                    pack(t + 1, ws, (vx, vz, sxx, szz, sxz))
                pressure = -0.5 * (sxx + szz)
                if w == 0:
                    rounded = pressure.astype(BF16).astype(F32)
                    for zc in range(zc_n):
                        srcf[t * shots + s, zc] = rounded[:, zc * LANES : (zc + 1) * LANES]
                else:
                    win[t, reach, s] = jnp.concatenate([pressure, slide_z - slide_x], 0).astype(BF16)
                return carry

            lax.fori_loop(0, shots, step, 0)
        if t < STEPS - 1:
            send_halo(t + 1)
        hop(t, 1)
        for k in range(2, reach + 1):
            if t - k + 1 >= 0:
                hop_wait(t - k + 1, k - 1)
                hop(t - k + 1, k)
        widen(t, reach)

    for late in range(1, reach + 1):
        for k in range(2, reach + 1):
            t = STEPS - 1 + late - k + 1
            if 0 <= t < STEPS:
                hop_wait(t, k - 1)
                hop(t, k)
    for t in range(STEPS):
        hop_wait(t, reach)
        for k in range(1, reach + 1):
            pl.when(me - k >= 0)(functools.partial(widen, t, reach - k))
            pl.when(me + k < n_slab)(functools.partial(widen, t, reach + k))

    scale = 1.0 / (shots * n_shot * STEPS)

    def correlate(owner):
        h0 = pl.multiple_of(owner * per, 8)

        def over_z(zc, carry):
            def over_ts(ts, sums):
                source = srcf[ts, zc]
                out = []
                for c in range(2):
                    for p in range(per + 1):
                        out.append(
                            sums[c * (per + 1) + p]
                            + source * wf[c, ts, zc, pl.ds(h0 + p, width), :])
                return tuple(out)

            sums = lax.fori_loop(
                0, STEPS * shots, over_ts,
                tuple(jnp.zeros((width, LANES), F32) for _ in range(2 * (per + 1))), unroll=2)
            at = pl.ds(pl.multiple_of(zc * LANES, LANES), LANES)
            for p in range(per):
                keep = off_ref[h0 + p] == h0 + p - SHIFT
                both = scale * jnp.concatenate(
                    [jnp.where(keep, sums[c * (per + 1) + p], sums[c * (per + 1) + p + 1])
                     for c in range(2)], 0)
                part[h0 + p, :, at] = both
                part_bf[h0 + p, :, at] = both.astype(BF16)
            return carry

        lax.fori_loop(0, zc_n, over_z, 0)

    def r1_copy(a):
        start = (2 * a + 1 - par) * per
        return pltpu.make_async_remote_copy(
            src_ref=part_bf.at[pl.ds(start, per)], dst_ref=r1.at[a],
            send_sem=r1_send.at[a], recv_sem=r1_recv.at[a],
            device_id={"shot": mate}, device_id_type=MESH)

    for q in range(1, na + 1):
        a = lax.rem(mine + q, na)
        correlate(2 * a + 1 - par)
        r1_copy(a).start()

    def r2_copy(q):
        a = lax.rem(mine + q, na)
        return pltpu.make_async_remote_copy(
            src_ref=s2.at[q - 1], dst_ref=r2.at[q - 1],
            send_sem=r2_send.at[q - 1], recv_sem=r2_recv.at[q - 1],
            device_id={"shot": 2 * a + par}, device_id_type=MESH)

    for q in range(1, na):
        a = lax.rem(mine + q, na)
        owner = 2 * a + par
        correlate(owner)
        r1_copy(a).wait_recv()

        def join(p, carry, a=a, owner=owner, q=q):
            s2[q - 1, p] = (part[owner * per + p] + r1[a, p].astype(F32)).astype(BF16)
            return carry

        lax.fori_loop(0, per, join, 0)
        r2_copy(q).start()
    correlate(shot)
    r1_copy(mine).wait_recv()
    for q in range(1, na):
        r2_copy(q).wait_recv()

    ratio = vs / vp
    coef = 2.0 * ratio * ratio
    rho_vp = 2.0 * rho * vp
    rho_vs = 2.0 * rho * vs

    def finish(p, carry):
        both = part[shot * per + p] + r1[mine, p].astype(F32)
        for q in range(1, na):
            both = both + r2[q - 1, p].astype(F32)
        pp = both[:width]
        ps = both[width:]
        ovp_ref[p] = rho_vp * pp
        ovs_ref[p] = rho_vs * (ps - coef * pp)
        orho_ref[p] = vp * vp * pp + vs * vs * ps
        return carry

    lax.fori_loop(0, per, finish, 0)

    for t in range(STEPS):
        pl.when(has_r)(lambda: halo_copy(t, True).wait_send())
        pl.when(has_l)(lambda: halo_copy(t, False).wait_send())
        for k in range(1, reach + 1):
            hop_done(t, k)
    pl.when(has_r)(lambda: rho_copy(True).wait_send())
    pl.when(has_l)(lambda: rho_copy(False).wait_send())
    for a in range(na):
        r1_copy(lax.rem(mine + a, na)).wait_send()
    for q in range(1, na):
        r2_copy(q).wait_send()


def shards(n_slab, n_shot, source_state, receiver_state, p_velocity, s_velocity, density,
           receiver_data, source_x, source_z, receiver_x, receiver_z, offsets):
    shots, _, width, depth = source_state.shape
    noff = offsets.shape[0]
    nrec = receiver_x.shape[0]
    span = SHIFT // width
    reach = min(span, n_slab - 1)
    per = noff // n_shot
    na = n_shot // 2
    rows = 2 * shots
    slots = 2 * reach + 1
    nz = depth // LANES
    ts = STEPS * shots
    vmem = pl.BlockSpec(memory_space=pltpu.VMEM)
    smem = pl.BlockSpec(memory_space=pltpu.SMEM)
    image = jax.ShapeDtypeStruct((per, width, depth), F32)
    state = jax.ShapeDtypeStruct(source_state.shape, F32)
    dma = pltpu.SemaphoreType.DMA
    return pl.pallas_call(
        functools.partial(kernel, n_slab, n_shot, reach, shots, noff),
        out_shape=(state, state, image, image, image),
        in_specs=[vmem] * 6 + [smem, smem, vmem, vmem, smem],
        out_specs=(vmem,) * 5,
        scratch_shapes=[
            pltpu.VMEM((4, width, depth), F32),
            pltpu.VMEM((ts * width, depth), F32),
            pltpu.VMEM((ts * width, nrec), F32),
            pltpu.VMEM((width, depth), F32),
            pltpu.VMEM((width, depth), F32),
            pltpu.VMEM((STEPS, 4, rows, depth), F32),
            pltpu.VMEM((STEPS, 3, rows, depth), F32),
            pltpu.VMEM((STEPS, 4, rows, depth), F32),
            pltpu.VMEM((STEPS, 3, rows, depth), F32),
            pltpu.VMEM((2, rows, depth), F32),
            pltpu.VMEM((ts, nz, width, LANES), F32),
            pltpu.VMEM((STEPS, slots, shots, 2 * width, depth), BF16),
            pltpu.VMEM((2, ts, nz, (2 * span + 1) * width, LANES), F32),
            pltpu.VMEM((noff, 2 * width, depth), F32),
            pltpu.VMEM((noff, 2 * width, depth), BF16),
            pltpu.VMEM((na, per, 2 * width, depth), BF16),
            pltpu.VMEM((na - 1, per, 2 * width, depth), BF16),
            pltpu.VMEM((na - 1, per, 2 * width, depth), BF16),
            dma((STEPS, 2)), dma((STEPS, 2)), dma((2,)), dma((2,)),
            dma((STEPS, slots)), dma((STEPS, slots)),
            dma((na,)), dma((na,)), dma((na - 1,)), dma((na - 1,)),
        ],
        compiler_params=pltpu.CompilerParams(
            collective_id=0, has_side_effects=True, vmem_limit_bytes=40 * 2**20),
    )(source_state, receiver_state, p_velocity, s_velocity, density, receiver_data,
      source_x, source_z, receiver_x.reshape(1, nrec), receiver_z.reshape(1, nrec), offsets)


def solution(mesh):
    return jax.shard_map(
        functools.partial(shards, mesh.shape["slab"], mesh.shape["shot"]),
        mesh=mesh,
        in_specs=(
            P(("group", "shot"), None, "slab", None),
            P(("group", "shot"), None, "slab", None),
            P(("group", "slab"), None),
            P(("group", "slab"), None),
            P(("group", "slab"), None),
            P(("group", "shot"), None, None),
            P(("group", "shot")),
            P(("group", "shot")),
            P("group"),
            P("group"),
            P(),
        ),
        out_specs=(
            P(("group", "shot"), None, "slab", None),
            P(("group", "shot"), None, "slab", None),
            P(("group", "shot"), "slab", None),
            P(("group", "shot"), "slab", None),
            P(("group", "shot"), "slab", None),
        ),
        check_vma=False,
    )
```

```python
import functools
import math

import jax
import jax.numpy as jnp
from jax import lax
from jax.experimental import pallas as pl
from jax.experimental.pallas import tpu as pltpu
from jax.sharding import PartitionSpec as P

STEPS = 4
SHIFT = 32
LANES = 128
DT = 0.3
DIRECT = ()
F32 = jnp.float32
BF16 = jnp.bfloat16
MESH = pl.DeviceIdType.MESH


def kernel(
    n_slab, n_shot, reach, shots, noff,
    src_in, rec_in, vp_in, vs_in, rho_in, data_in, sx_ref, sz_ref, rx_in, rz_in, off_ref,
    fs_ref, fr_ref, ovp_ref, ovs_ref, orho_ref,
    src_ref, rec_ref, vp_ref, vs_ref, rho_ref, data_ref, rx_ref, rz_ref, in_sem,
    model, inj, spread, rho_l, rho_r, to_r, to_l, from_l, from_r, edge, srcf, win, wf,
    part, part_bf, r1, s2, r2,
    halo_send, halo_recv, rho_send, rho_recv, win_send, win_recv, r1_send, r1_recv, r2_send, r2_recv,
):
    width, depth = rho_ref.shape
    zc_n = depth // LANES
    per = noff // n_shot
    na = n_shot // 2
    span = SHIFT // width
    me = lax.axis_index("slab")
    shot = lax.axis_index("shot")
    par = lax.rem(shot, 2)
    mate = shot + 1 - 2 * par
    mine = shot // 2
    has_l = me > 0
    has_r = me < n_slab - 1

    inward = [
        pltpu.make_async_copy(a, b, in_sem.at[i])
        for i, (a, b) in enumerate((
            (src_in, src_ref), (rec_in, rec_ref), (rho_in, rho_ref), (vp_in, vp_ref), (vs_in, vs_ref),
            (data_in, data_ref), (rx_in, rx_ref), (rz_in, rz_ref)))
    ]
    for copy in inward:
        copy.start()

    barrier = pltpu.get_barrier_semaphore()

    def greet(axis, index):
        pl.semaphore_signal(barrier, inc=1, device_id={axis: index}, device_id_type=MESH)

    for k in range(1, reach + 1):
        pl.when(me - k >= 0)(functools.partial(greet, "slab", me - k))
        pl.when(me + k < n_slab)(functools.partial(greet, "slab", me + k))
    greet("shot", mate)
    for q in range(1, na):
        greet("shot", 2 * lax.rem(mine + q, na) + par)

    row = lax.broadcasted_iota(jnp.int32, (width, depth), 0)
    lane = lax.broadcasted_iota(jnp.int32, (width, depth), 1)

    def back_z(f):
        return f - jnp.where(lane == 0, 0.0, pltpu.roll(f, 1, 1))

    def fore_z(f):
        return jnp.where(lane == depth - 1, 0.0, pltpu.roll(f, depth - 1, 1)) - f

    def down(f, halo):
        return jnp.where(row == 0, halo, pltpu.roll(f, 1, 0))

    def up(f, halo):
        return jnp.where(row == width - 1, halo, pltpu.roll(f, width - 1, 0))

    def pack(t, ws, fields):
        vx, vz, sxx, szz, sxz = fields
        one = pl.ds(ws, 1)
        for slot, f in enumerate((sxx, szz, sxz, vz)):
            to_r[t, slot, one, :] = f[width - 1 : width, :]
        for slot, f in enumerate((vx, sxx, sxz)):
            to_l[t, slot, one, :] = f[0:1, :]

    for copy in inward:
        copy.wait()
    for w, ref in enumerate((src_ref, rec_ref)):

        def first(s, carry, w=w, ref=ref):
            pack(0, w * shots + s, [ref[s, i] for i in range(5)])
            return carry

        lax.fori_loop(0, shots, first, 0, unroll=True)

    count = sum(
        (me - k >= 0).astype(jnp.int32) + (me + k < n_slab).astype(jnp.int32)
        for k in range(1, reach + 1)
    ) + na
    pl.semaphore_wait(barrier, count)

    def halo_copy(t, right):
        if right:
            return pltpu.make_async_remote_copy(
                src_ref=to_r.at[t], dst_ref=from_l.at[t],
                send_sem=halo_send.at[t, 0], recv_sem=halo_recv.at[t, 0],
                device_id={"slab": me + 1}, device_id_type=MESH)
        return pltpu.make_async_remote_copy(
            src_ref=to_l.at[t], dst_ref=from_r.at[t],
            send_sem=halo_send.at[t, 1], recv_sem=halo_recv.at[t, 1],
            device_id={"slab": me - 1}, device_id_type=MESH)

    def rho_copy(right):
        if right:
            return pltpu.make_async_remote_copy(
                src_ref=rho_ref, dst_ref=rho_l, send_sem=rho_send.at[0], recv_sem=rho_recv.at[0],
                device_id={"slab": me + 1}, device_id_type=MESH)
        return pltpu.make_async_remote_copy(
            src_ref=rho_ref, dst_ref=rho_r, send_sem=rho_send.at[1], recv_sem=rho_recv.at[1],
            device_id={"slab": me - 1}, device_id_type=MESH)

    def send_halo(t):
        pl.when(has_r)(lambda: halo_copy(t, True).start())
        pl.when(has_l)(lambda: halo_copy(t, False).start())

    send_halo(0)
    pl.when(has_r)(lambda: rho_copy(True).start())
    pl.when(has_l)(lambda: rho_copy(False).start())

    def win_copy(t, from_slot, to_slot, target):
        return pltpu.make_async_remote_copy(
            src_ref=win.at[t, from_slot], dst_ref=win.at[t, to_slot],
            send_sem=win_send.at[t, to_slot], recv_sem=win_recv.at[t, to_slot],
            device_id={"slab": target}, device_id_type=MESH)

    def sides(t, k):
        if t in DIRECT:
            return (
                (me + k < n_slab, me - k >= 0, win_copy(t, reach, reach - k, me + k)),
                (me - k >= 0, me + k < n_slab, win_copy(t, reach, reach + k, me - k)),
            )
        return (
            (has_r & (me - k + 1 >= 0), me - k >= 0, win_copy(t, reach - k + 1, reach - k, me + 1)),
            (has_l & (me + k - 1 < n_slab), me + k < n_slab, win_copy(t, reach + k - 1, reach + k, me - 1)),
        )

    arrived = set()

    def hop_wait(t, k):
        if k > 0 and (t, k) not in arrived:
            arrived.add((t, k))
            for _, receives, copy in sides(t, k):
                pl.when(receives)(copy.wait_recv)

    def hop(t, k):
        if t not in DIRECT:
            hop_wait(t, k - 1)
        for sends, _, copy in sides(t, k):
            pl.when(sends)(copy.start)

    def hop_done(t, k):
        for sends, _, copy in sides(t, k):
            pl.when(sends)(copy.wait_send)

    rho = rho_ref[...]
    vp = vp_ref[...]
    vs = vs_ref[...]
    shear = rho * vs * vs
    lame = rho * (vp * vp - 2.0 * vs * vs)
    model[0] = 1.0 / rho
    model[1] = shear
    model[2] = lame
    model[3] = lame + 2.0 * shear

    @pl.when(jnp.logical_not(has_l))
    def _():
        from_l[...] = jnp.zeros_like(from_l)
        rho_l[...] = jnp.ones_like(rho_l)

    @pl.when(jnp.logical_not(has_r))
    def _():
        from_r[...] = jnp.zeros_like(from_r)
        rho_r[...] = jnp.ones_like(rho_r)

    nrec = data_ref.shape[2]
    rel = rx_ref[...] - me * width
    at_x = rel == lax.broadcasted_iota(jnp.int32, (width, nrec), 0)
    for s in range(shots):
        for t in range(STEPS):
            spread[pl.ds((t * shots + s) * width, width), :] = jnp.where(
                at_x, data_ref[s, t : t + 1, :], 0.0)
    at_z = jnp.where(
        lax.broadcasted_iota(jnp.int32, (depth, nrec), 0) == rz_ref[...], 1.0, 0.0).astype(BF16)
    rest = spread[...]
    total = None
    for _ in range(3):
        piece = rest.astype(BF16)
        rest = rest - piece.astype(F32)
        term = lax.dot_general(piece, at_z, (((1,), (1,)), ((), ())), preferred_element_type=F32)
        total = term if total is None else total + term
    inj[...] = total

    def zero(i, carry):
        wf[0, i] = jnp.zeros(wf.shape[2:], F32)
        wf[1, i] = jnp.zeros(wf.shape[2:], F32)
        return carry

    lax.fori_loop(0, STEPS * shots, zero, 0, unroll=2)

    sign_rows = jnp.where(row < shots, DT, -DT)

    def widen(t, slot):
        base = (slot - reach + span) * width

        def body(s, carry):
            both = win[t, slot, s].astype(F32)
            for zc in range(zc_n):
                cut = both[:, zc * LANES : (zc + 1) * LANES]
                wf[0, t * shots + s, zc, base : base + width, :] = cut[:width]
                wf[1, t * shots + s, zc, base : base + width, :] = cut[width:]
            return carry

        lax.fori_loop(0, shots, body, 0, unroll=True)

    for t in range(STEPS):
        pl.when(has_l)(lambda: halo_copy(t, True).wait_recv())
        pl.when(has_r)(lambda: halo_copy(t, False).wait_recv())
        if t == 0:
            pl.when(has_l)(lambda: rho_copy(True).wait_recv())
            pl.when(has_r)(lambda: rho_copy(False).wait_recv())
        buoy_l = jnp.where(has_l, 1.0 / rho_l[width - 1 : width, :], 0.0)
        buoy_r = jnp.where(has_r, 1.0 / rho_r[0:1, :], 0.0)
        edge[0] = from_l[t, 3] + sign_rows * buoy_l * (
            to_l[t, 2] - from_l[t, 2] + fore_z(from_l[t, 1]))
        edge[1] = from_r[t, 0] + sign_rows * buoy_r * (
            from_r[t, 1] - to_r[t, 0] + back_z(from_r[t, 2]))
        wavelet = 2.0 * math.cos(1.3 * t + 0.4)
        for w in range(2):
            state = (fs_ref, fr_ref)[w]
            before = ((src_ref, rec_ref)[w]) if t == 0 else state
            sg = (DT, -DT)[w]

            def step(s, carry, w=w, state=state, before=before, sg=sg, t=t, wavelet=wavelet):
                ws = w * shots + s
                one = pl.ds(ws, 1)
                vx, vz, sxx, szz, sxz = [before[s, i] for i in range(5)]
                buoy = sg * model[0]
                vx = vx + buoy * (sxx - down(sxx, from_l[t, 0, one, :]) + back_z(sxz))
                vz = vz + buoy * (up(sxz, from_r[t, 2, one, :]) - sxz + fore_z(szz))
                stretch = sg * (up(vx, edge[1, one, :]) - vx)
                squeeze = sg * back_z(vz)
                slide_x = vz - down(vz, edge[0, one, :])
                slide_z = fore_z(vx)
                if w == 0:
                    here = (row + me * width == sx_ref[s]) & (lane == sz_ref[s])
                    add = jnp.where(here, wavelet, 0.0)
                else:
                    start = pl.multiple_of((t * shots + s) * width, width)
                    add = inj[pl.ds(start, width), :]
                sxx = sxx + (model[3] * stretch + model[2] * squeeze) + add
                szz = szz + (model[2] * stretch + model[3] * squeeze) + add
                sxz = sxz + sg * model[1] * (slide_x + slide_z)
                for i, f in enumerate((vx, vz, sxx, szz, sxz)):
                    state[s, i] = f
                if t < STEPS - 1:
                    pack(t + 1, ws, (vx, vz, sxx, szz, sxz))
                pressure = -0.5 * (sxx + szz)
                if w == 0:
                    rounded = pressure.astype(BF16).astype(F32)
                    for zc in range(zc_n):
                        srcf[t * shots + s, zc] = rounded[:, zc * LANES : (zc + 1) * LANES]
                else:
                    win[t, reach, s] = jnp.concatenate([pressure, slide_z - slide_x], 0).astype(BF16)
                return carry

            lax.fori_loop(0, shots, step, 0, unroll=True)
        if t < STEPS - 1:
            send_halo(t + 1)
        if t in DIRECT:
            for k in range(1, reach + 1):
                hop(t, k)
        else:
            hop(t, 1)
        for k in range(2, reach + 1):
            if t - k + 1 >= 0 and t - k + 1 not in DIRECT:
                hop(t - k + 1, k)
        widen(t, reach)

    def take(t, low, high):
        for k in range(low, high + 1):
            hop_wait(t, k)
            pl.when(me - k >= 0)(functools.partial(widen, t, reach - k))
            pl.when(me + k < n_slab)(functools.partial(widen, t, reach + k))

    scale = 1.0 / (shots * n_shot * STEPS)

    def correlate(t, owner):
        h0 = pl.multiple_of(owner * per, 8)

        def over_z(zc, carry):
            sums = [None] * (2 * (per + 1))
            for s in range(shots):
                source = srcf[t * shots + s, zc]
                for c in range(2):
                    for p in range(per + 1):
                        term = source * wf[c, t * shots + s, zc, pl.ds(h0 + p, width), :]
                        i = c * (per + 1) + p
                        sums[i] = term if s == 0 else sums[i] + term
            at = pl.ds(pl.multiple_of(zc * LANES, LANES), LANES)
            for p in range(per):
                keep = off_ref[h0 + p] == h0 + p - SHIFT
                both = scale * jnp.concatenate(
                    [jnp.where(keep, sums[c * (per + 1) + p], sums[c * (per + 1) + p + 1])
                     for c in range(2)], 0)
                if t > 0:
                    both = both + part[h0 + p, :, at]
                part[h0 + p, :, at] = both
                if t == STEPS - 1:
                    part_bf[h0 + p, :, at] = both.astype(BF16)
            return carry

        lax.fori_loop(0, zc_n, over_z, 0)

    def all_owners(t):
        def body(owner, carry):
            correlate(t, owner)
            return carry

        lax.fori_loop(0, n_shot, body, 0)

    for t in range(STEPS - 1):
        take(t, 1, reach)
        all_owners(t)
        for k in range(2, reach + 1):
            later = STEPS + t - k + 1
            if 0 <= later < STEPS and later not in DIRECT:
                hop(later, k)
    for late in range(STEPS, STEPS + reach):
        for k in range(2, reach + 1):
            later = late + STEPS - 1 - k + 1
            if 0 <= later < STEPS and later not in DIRECT:
                hop(later, k)

    def r1_copy(a):
        start = (2 * a + 1 - par) * per
        return pltpu.make_async_remote_copy(
            src_ref=part_bf.at[pl.ds(start, per)], dst_ref=r1.at[a],
            send_sem=r1_send.at[a], recv_sem=r1_recv.at[a],
            device_id={"shot": mate}, device_id_type=MESH)

    def r2_copy(a):
        q = lax.rem(a - mine + na, na)
        return pltpu.make_async_remote_copy(
            src_ref=s2.at[q - 1], dst_ref=r2.at[q - 1],
            send_sem=r2_send.at[q - 1], recv_sem=r2_recv.at[q - 1],
            device_id={"shot": 2 * a + par}, device_id_type=MESH)

    last = STEPS - 1
    near = min(reach, -(-per // width)) if na == 2 else reach
    take(last, 1, near)
    for turn in range(na):
        if turn == 1:
            take(last, near + 1, reach)
        ahead = lax.rem(turn + par, na)
        correlate(last, 2 * ahead + 1 - par)
        r1_copy(ahead).start()
        a = lax.rem(turn + 1 - par, na)
        owner = 2 * a + par
        correlate(last, owner)
        r1_copy(a).wait_recv()

        @pl.when(a != mine)
        def _(a=a, owner=owner):
            q = lax.rem(a - mine + na, na)

            def join(p, carry):
                s2[q - 1, p] = (part[owner * per + p] + r1[a, p].astype(F32)).astype(BF16)
                return carry

            lax.fori_loop(0, per, join, 0, unroll=4)
            r2_copy(a).start()

    for q in range(1, na):
        r2_copy(lax.rem(mine + q, na)).wait_recv()

    ratio = vs / vp
    coef = 2.0 * ratio * ratio
    rho_vp = 2.0 * rho * vp
    rho_vs = 2.0 * rho * vs

    def finish(p, carry):
        both = part[shot * per + p] + r1[mine, p].astype(F32)
        for q in range(1, na):
            both = both + r2[q - 1, p].astype(F32)
        pp = both[:width]
        ps = both[width:]
        ovp_ref[p] = rho_vp * pp
        ovs_ref[p] = rho_vs * (ps - coef * pp)
        orho_ref[p] = vp * vp * pp + vs * vs * ps
        return carry

    lax.fori_loop(0, per, finish, 0, unroll=4)

    for t in range(STEPS):
        pl.when(has_r)(lambda: halo_copy(t, True).wait_send())
        pl.when(has_l)(lambda: halo_copy(t, False).wait_send())
        for k in range(1, reach + 1):
            hop_done(t, k)
    pl.when(has_r)(lambda: rho_copy(True).wait_send())
    pl.when(has_l)(lambda: rho_copy(False).wait_send())
    for a in range(na):
        r1_copy(lax.rem(mine + a, na)).wait_send()
    for q in range(1, na):
        r2_copy(lax.rem(mine + q, na)).wait_send()


def store(*refs):
    copies = [
        pltpu.make_async_copy(refs[i], refs[5 + i], refs[10].at[i]) for i in range(5)]
    for copy in copies:
        copy.start()
    for copy in copies:
        copy.wait()


def shards(n_slab, n_shot, source_state, receiver_state, p_velocity, s_velocity, density,
           receiver_data, source_x, source_z, receiver_x, receiver_z, offsets):
    shots, _, width, depth = source_state.shape
    noff = offsets.shape[0]
    nrec = receiver_x.shape[0]
    span = SHIFT // width
    reach = min(span, n_slab - 1)
    per = noff // n_shot
    na = n_shot // 2
    rows = 2 * shots
    slots = 2 * reach + 1
    nz = depth // LANES
    ts = STEPS * shots
    vmem = pl.BlockSpec(memory_space=pltpu.VMEM)
    hbm = pl.BlockSpec(memory_space=pltpu.HBM)
    smem = pl.BlockSpec(memory_space=pltpu.SMEM)
    image = jax.ShapeDtypeStruct((per, width, depth), F32)
    state = jax.ShapeDtypeStruct(source_state.shape, F32)
    dma = pltpu.SemaphoreType.DMA
    results = pl.pallas_call(
        functools.partial(kernel, n_slab, n_shot, reach, shots, noff),
        out_shape=(state, state, image, image, image),
        in_specs=[hbm] * 6 + [smem, smem, hbm, hbm, smem],
        out_specs=(vmem,) * 5,
        scratch_shapes=[
            pltpu.VMEM(source_state.shape, F32),
            pltpu.VMEM(source_state.shape, F32),
            pltpu.VMEM((width, depth), F32),
            pltpu.VMEM((width, depth), F32),
            pltpu.VMEM((width, depth), F32),
            pltpu.VMEM(receiver_data.shape, F32),
            pltpu.VMEM((1, nrec), jnp.int32),
            pltpu.VMEM((1, nrec), jnp.int32),
            dma((8,)),
            pltpu.VMEM((4, width, depth), F32),
            pltpu.VMEM((ts * width, depth), F32),
            pltpu.VMEM((ts * width, nrec), F32),
            pltpu.VMEM((width, depth), F32),
            pltpu.VMEM((width, depth), F32),
            pltpu.VMEM((STEPS, 4, rows, depth), F32),
            pltpu.VMEM((STEPS, 3, rows, depth), F32),
            pltpu.VMEM((STEPS, 4, rows, depth), F32),
            pltpu.VMEM((STEPS, 3, rows, depth), F32),
            pltpu.VMEM((2, rows, depth), F32),
            pltpu.VMEM((ts, nz, width, LANES), F32),
            pltpu.VMEM((STEPS, slots, shots, 2 * width, depth), BF16),
            pltpu.VMEM((2, ts, nz, (2 * span + 1) * width, LANES), F32),
            pltpu.VMEM((noff, 2 * width, depth), F32),
            pltpu.VMEM((noff, 2 * width, depth), BF16),
            pltpu.VMEM((na, per, 2 * width, depth), BF16),
            pltpu.VMEM((na - 1, per, 2 * width, depth), BF16),
            pltpu.VMEM((na - 1, per, 2 * width, depth), BF16),
            dma((STEPS, 2)), dma((STEPS, 2)), dma((2,)), dma((2,)),
            dma((STEPS, slots)), dma((STEPS, slots)),
            dma((na,)), dma((na,)), dma((na - 1,)), dma((na - 1,)),
        ],
        compiler_params=pltpu.CompilerParams(
            collective_id=0, has_side_effects=True, vmem_limit_bytes=61 * 2**20),
    )(source_state, receiver_state, p_velocity, s_velocity, density, receiver_data,
      source_x, source_z, receiver_x.reshape(1, nrec), receiver_z.reshape(1, nrec), offsets)
    return pl.pallas_call(
        store,
        out_shape=(state, state, image, image, image),
        in_specs=[vmem] * 5,
        out_specs=(hbm,) * 5,
        scratch_shapes=[dma((5,))],
    )(*results)


def solution(mesh):
    return jax.shard_map(
        functools.partial(shards, mesh.shape["slab"], mesh.shape["shot"]),
        mesh=mesh,
        in_specs=(
            P(("group", "shot"), None, "slab", None),
            P(("group", "shot"), None, "slab", None),
            P(("group", "slab"), None),
            P(("group", "slab"), None),
            P(("group", "slab"), None),
            P(("group", "shot"), None, None),
            P(("group", "shot")),
            P(("group", "shot")),
            P("group"),
            P("group"),
            P(),
        ),
        out_specs=(
            P(("group", "shot"), None, "slab", None),
            P(("group", "shot"), None, "slab", None),
            P(("group", "shot"), "slab", None),
            P(("group", "shot"), "slab", None),
            P(("group", "shot"), "slab", None),
        ),
        check_vma=False,
    )
```

```python
import functools
import math

import jax
import jax.numpy as jnp
from jax import lax
from jax.experimental import pallas as pl
from jax.experimental.pallas import tpu as pltpu
from jax.sharding import PartitionSpec as P

STEPS = 4
SHIFT = 32
LANES = 128
DT = 0.3
F32 = jnp.float32
BF16 = jnp.bfloat16
MESH = pl.DeviceIdType.MESH


def kernel(
    n_slab, n_shot, reach, shots, noff,
    src_in, rec_in, vp_in, vs_in, rho_in, data_in, sx_ref, sz_ref, rx_in, rz_in, off_ref,
    fs_ref, fr_ref, ovp_ref, ovs_ref, orho_ref,
    src_ref, rec_ref, vp_ref, vs_ref, rho_ref, data_ref, rx_ref, rz_ref, in_sem,
    model, inj, spread, rho_l, rho_r, to_r, to_l, from_l, from_r, edge, srcf, win, wf,
    part, part_bf, r1, s2, r2,
    halo_send, halo_recv, rho_send, rho_recv, win_send, win_recv, r1_send, r1_recv, r2_send, r2_recv,
):
    width, depth = rho_ref.shape
    zc_n = depth // LANES
    per = noff // n_shot
    na = n_shot // 2
    span = SHIFT // width
    me = lax.axis_index("slab")
    shot = lax.axis_index("shot")
    par = lax.rem(shot, 2)
    mate = shot + 1 - 2 * par
    mine = shot // 2
    has_l = me > 0
    has_r = me < n_slab - 1

    inward = [
        pltpu.make_async_copy(a, b, in_sem.at[i])
        for i, (a, b) in enumerate((
            (src_in, src_ref), (rec_in, rec_ref), (rho_in, rho_ref), (vp_in, vp_ref), (vs_in, vs_ref),
            (data_in, data_ref), (rx_in, rx_ref), (rz_in, rz_ref)))
    ]
    for copy in inward:
        copy.start()

    barrier = pltpu.get_barrier_semaphore()

    def greet(axis, index):
        pl.semaphore_signal(barrier, inc=1, device_id={axis: index}, device_id_type=MESH)

    for k in range(1, reach + 1):
        pl.when(me - k >= 0)(functools.partial(greet, "slab", me - k))
        pl.when(me + k < n_slab)(functools.partial(greet, "slab", me + k))
    greet("shot", mate)
    for q in range(1, na):
        greet("shot", 2 * lax.rem(mine + q, na) + par)

    row = lax.broadcasted_iota(jnp.int32, (width, depth), 0)
    lane = lax.broadcasted_iota(jnp.int32, (width, depth), 1)

    def back_z(f):
        return f - jnp.where(lane == 0, 0.0, pltpu.roll(f, 1, 1))

    def fore_z(f):
        return jnp.where(lane == depth - 1, 0.0, pltpu.roll(f, depth - 1, 1)) - f

    def down(f, halo):
        return jnp.where(row == 0, halo, pltpu.roll(f, 1, 0))

    def up(f, halo):
        return jnp.where(row == width - 1, halo, pltpu.roll(f, width - 1, 0))

    def pack(t, ws, fields):
        vx, vz, sxx, szz, sxz = fields
        one = pl.ds(ws, 1)
        for slot, f in enumerate((sxx, szz, sxz, vz)):
            to_r[t, slot, one, :] = f[width - 1 : width, :]
        for slot, f in enumerate((vx, sxx, sxz)):
            to_l[t, slot, one, :] = f[0:1, :]

    for copy in inward:
        copy.wait()
    for w, ref in enumerate((src_ref, rec_ref)):

        def first(s, carry, w=w, ref=ref):
            pack(0, w * shots + s, [ref[s, i] for i in range(5)])
            return carry

        lax.fori_loop(0, shots, first, 0, unroll=True)

    count = sum(
        (me - k >= 0).astype(jnp.int32) + (me + k < n_slab).astype(jnp.int32)
        for k in range(1, reach + 1)
    ) + na
    pl.semaphore_wait(barrier, count)

    def halo_copy(t, right):
        if right:
            return pltpu.make_async_remote_copy(
                src_ref=to_r.at[t], dst_ref=from_l.at[t],
                send_sem=halo_send.at[t, 0], recv_sem=halo_recv.at[t, 0],
                device_id={"slab": me + 1}, device_id_type=MESH)
        return pltpu.make_async_remote_copy(
            src_ref=to_l.at[t], dst_ref=from_r.at[t],
            send_sem=halo_send.at[t, 1], recv_sem=halo_recv.at[t, 1],
            device_id={"slab": me - 1}, device_id_type=MESH)

    def rho_copy(right):
        if right:
            return pltpu.make_async_remote_copy(
                src_ref=rho_ref, dst_ref=rho_l, send_sem=rho_send.at[0], recv_sem=rho_recv.at[0],
                device_id={"slab": me + 1}, device_id_type=MESH)
        return pltpu.make_async_remote_copy(
            src_ref=rho_ref, dst_ref=rho_r, send_sem=rho_send.at[1], recv_sem=rho_recv.at[1],
            device_id={"slab": me - 1}, device_id_type=MESH)

    def send_halo(t):
        pl.when(has_r)(lambda: halo_copy(t, True).start())
        pl.when(has_l)(lambda: halo_copy(t, False).start())

    send_halo(0)
    pl.when(has_r)(lambda: rho_copy(True).start())
    pl.when(has_l)(lambda: rho_copy(False).start())

    def win_copy(t, from_slot, to_slot, target):
        return pltpu.make_async_remote_copy(
            src_ref=win.at[t, from_slot], dst_ref=win.at[t, to_slot],
            send_sem=win_send.at[t, to_slot], recv_sem=win_recv.at[t, to_slot],
            device_id={"slab": target}, device_id_type=MESH)

    def sides(t, k):
        return (
            (has_r & (me - k + 1 >= 0), me - k >= 0, win_copy(t, reach - k + 1, reach - k, me + 1)),
            (has_l & (me + k - 1 < n_slab), me + k < n_slab, win_copy(t, reach + k - 1, reach + k, me - 1)),
        )

    arrived = set()

    def hop_wait(t, k):
        if k > 0 and (t, k) not in arrived:
            arrived.add((t, k))
            for _, receives, copy in sides(t, k):
                pl.when(receives)(copy.wait_recv)

    def hop(t, k):
        hop_wait(t, k - 1)
        for sends, _, copy in sides(t, k):
            pl.when(sends)(copy.start)

    def hop_done(t, k):
        for sends, _, copy in sides(t, k):
            pl.when(sends)(copy.wait_send)

    rho = rho_ref[...]
    vp = vp_ref[...]
    vs = vs_ref[...]
    shear = rho * vs * vs
    lame = rho * (vp * vp - 2.0 * vs * vs)
    model[0] = 1.0 / rho
    model[1] = shear
    model[2] = lame
    model[3] = lame + 2.0 * shear

    @pl.when(jnp.logical_not(has_l))
    def _():
        from_l[...] = jnp.zeros_like(from_l)
        rho_l[...] = jnp.ones_like(rho_l)

    @pl.when(jnp.logical_not(has_r))
    def _():
        from_r[...] = jnp.zeros_like(from_r)
        rho_r[...] = jnp.ones_like(rho_r)

    nrec = data_ref.shape[2]
    rel = rx_ref[...] - me * width
    at_x = rel == lax.broadcasted_iota(jnp.int32, (width, nrec), 0)
    for s in range(shots):
        for t in range(STEPS):
            spread[pl.ds((t * shots + s) * width, width), :] = jnp.where(
                at_x, data_ref[s, t : t + 1, :], 0.0)
    at_z = jnp.where(
        lax.broadcasted_iota(jnp.int32, (depth, nrec), 0) == rz_ref[...], 1.0, 0.0).astype(BF16)
    rest = spread[...]
    total = None
    for _ in range(3):
        piece = rest.astype(BF16)
        rest = rest - piece.astype(F32)
        term = lax.dot_general(piece, at_z, (((1,), (1,)), ((), ())), preferred_element_type=F32)
        total = term if total is None else total + term
    inj[...] = total

    def zero(i, carry):
        wf[0, i] = jnp.zeros(wf.shape[2:], F32)
        wf[1, i] = jnp.zeros(wf.shape[2:], F32)
        some = pl.ds(i * (noff // (STEPS * shots)), noff // (STEPS * shots))
        part[some] = jnp.zeros((noff // (STEPS * shots),) + part.shape[1:], F32)
        part_bf[some] = jnp.zeros((noff // (STEPS * shots),) + part.shape[1:], BF16)
        return carry

    lax.fori_loop(0, STEPS * shots, zero, 0, unroll=2)

    sign_rows = jnp.where(row < shots, DT, -DT)

    def widen(t, slot):
        base = (slot - reach + span) * width

        def body(s, carry):
            both = win[t, slot, s].astype(F32)
            for zc in range(zc_n):
                cut = both[:, zc * LANES : (zc + 1) * LANES]
                wf[0, t * shots + s, zc, base : base + width, :] = cut[:width]
                wf[1, t * shots + s, zc, base : base + width, :] = cut[width:]
            return carry

        lax.fori_loop(0, shots, body, 0, unroll=True)

    def take(t, k):
        hop_wait(t, k)
        pl.when(me - k >= 0)(functools.partial(widen, t, reach - k))
        pl.when(me + k < n_slab)(functools.partial(widen, t, reach + k))

    scale = 1.0 / (shots * n_shot * STEPS)
    last = STEPS - 1

    def correlate(t, group):
        h0 = pl.multiple_of(group * width, 8)
        slab = me + group - span

        def over_z(zc, carry):
            sums = [None] * (2 * (width + 1))
            for s in range(shots):
                source = srcf[t * shots + s, zc]
                for c in range(2):
                    for p in range(width + 1):
                        term = source * wf[c, t * shots + s, zc, pl.ds(h0 + p, width), :]
                        i = c * (width + 1) + p
                        sums[i] = term if s == 0 else sums[i] + term
            at = pl.ds(pl.multiple_of(zc * LANES, LANES), LANES)
            for p in range(width):
                keep = off_ref[h0 + p] == h0 + p - SHIFT
                both = scale * jnp.concatenate(
                    [jnp.where(keep, sums[c * (width + 1) + p], sums[c * (width + 1) + p + 1])
                     for c in range(2)], 0)
                if t > 0:
                    both = both + part[h0 + p, :, at]
                part[h0 + p, :, at] = both
                if t == last:
                    part_bf[h0 + p, :, at] = both.astype(BF16)
            return carry

        @pl.when((slab + 1 >= 0) & (slab < n_slab))
        def _():
            lax.fori_loop(0, zc_n, over_z, 0)

    def pair(t, k):
        def body(i, carry):
            correlate(t, span - k + i * (2 * k - 1))
            return carry

        lax.fori_loop(0, 2, body, 0)

    halves = per // width

    def own_group(k):
        low, high = span - k, span + k - 1
        odd = (low // halves) % 2
        return jnp.where(par == odd, low, high), jnp.where(par == odd, high, low)

    def r1_copy(k):
        return pltpu.make_async_remote_copy(
            src_ref=part_bf.at[pl.ds(own_group(k)[1] * width, width)], dst_ref=r1.at[k - 1],
            send_sem=r1_send.at[k - 1], recv_sem=r1_recv.at[k - 1],
            device_id={"shot": mate}, device_id_type=MESH)

    def r2_copy(k, q, target):
        return pltpu.make_async_remote_copy(
            src_ref=s2.at[k - 1], dst_ref=r2.at[q - 1, k - 1],
            send_sem=r2_send.at[k - 1], recv_sem=r2_recv.at[q - 1, k - 1],
            device_id={"shot": target}, device_id_type=MESH)

    def owner_of(k):
        owner = own_group(k)[0] // halves
        return owner, lax.rem(owner // 2 - mine + na, na)

    def begin(k):
        own, other = own_group(k)
        correlate(last, other)
        r1_copy(k).start()
        return own

    def join(k):
        r1_copy(k).wait_recv()
        owner, q = owner_of(k)
        own = own_group(k)[0]

        @pl.when(owner != shot)
        def _():
            def body(p, carry):
                s2[k - 1, p] = (part[own * width + p] + r1[k - 1, p].astype(F32)).astype(BF16)
                return carry

            lax.fori_loop(0, width, body, 0, unroll=True)
            r2_copy(k, q, owner).start()

    def advance(v):
        for k in range(2, reach + 1):
            if 0 <= v - k + 1 <= last:
                hop(v - k + 1, k)
        levels = []
        for k in range(1, span + 1):
            t = v - min(k, reach)
            if 0 <= t <= last:
                if k <= reach:
                    take(t, k)
                if t == last:
                    levels.append(k)
                else:
                    pair(t, k)
        for k in levels:
            begin(k)
        if v - 1 > last:
            for k in range(1, span + 1):
                if v - 1 - min(k, reach) == last:
                    join(k)
        for k in levels:
            correlate(last, own_group(k)[0])

    for t in range(STEPS):
        pl.when(has_l)(lambda: halo_copy(t, True).wait_recv())
        pl.when(has_r)(lambda: halo_copy(t, False).wait_recv())
        if t == 0:
            pl.when(has_l)(lambda: rho_copy(True).wait_recv())
            pl.when(has_r)(lambda: rho_copy(False).wait_recv())
        buoy_l = jnp.where(has_l, 1.0 / rho_l[width - 1 : width, :], 0.0)
        buoy_r = jnp.where(has_r, 1.0 / rho_r[0:1, :], 0.0)
        edge[0] = from_l[t, 3] + sign_rows * buoy_l * (
            to_l[t, 2] - from_l[t, 2] + fore_z(from_l[t, 1]))
        edge[1] = from_r[t, 0] + sign_rows * buoy_r * (
            from_r[t, 1] - to_r[t, 0] + back_z(from_r[t, 2]))
        wavelet = 2.0 * math.cos(1.3 * t + 0.4)
        for w in range(2):
            state = (fs_ref, fr_ref)[w]
            before = ((src_ref, rec_ref)[w]) if t == 0 else state
            sg = (DT, -DT)[w]

            def step(s, carry, w=w, state=state, before=before, sg=sg, t=t, wavelet=wavelet):
                ws = w * shots + s
                one = pl.ds(ws, 1)
                vx, vz, sxx, szz, sxz = [before[s, i] for i in range(5)]
                buoy = sg * model[0]
                vx = vx + buoy * (sxx - down(sxx, from_l[t, 0, one, :]) + back_z(sxz))
                vz = vz + buoy * (up(sxz, from_r[t, 2, one, :]) - sxz + fore_z(szz))
                stretch = sg * (up(vx, edge[1, one, :]) - vx)
                squeeze = sg * back_z(vz)
                slide_x = vz - down(vz, edge[0, one, :])
                slide_z = fore_z(vx)
                if w == 0:
                    here = (row + me * width == sx_ref[s]) & (lane == sz_ref[s])
                    add = jnp.where(here, wavelet, 0.0)
                else:
                    start = pl.multiple_of((t * shots + s) * width, width)
                    add = inj[pl.ds(start, width), :]
                sxx = sxx + (model[3] * stretch + model[2] * squeeze) + add
                szz = szz + (model[2] * stretch + model[3] * squeeze) + add
                sxz = sxz + sg * model[1] * (slide_x + slide_z)
                for i, f in enumerate((vx, vz, sxx, szz, sxz)):
                    state[s, i] = f
                if t < STEPS - 1:
                    pack(t + 1, ws, (vx, vz, sxx, szz, sxz))
                pressure = -0.5 * (sxx + szz)
                if w == 0:
                    rounded = pressure.astype(BF16).astype(F32)
                    for zc in range(zc_n):
                        srcf[t * shots + s, zc] = rounded[:, zc * LANES : (zc + 1) * LANES]
                else:
                    win[t, reach, s] = jnp.concatenate([pressure, slide_z - slide_x], 0).astype(BF16)
                return carry

            lax.fori_loop(0, shots, step, 0, unroll=True)
        if t < STEPS - 1:
            send_halo(t + 1)
        hop(t, 1)
        widen(t, reach)
        advance(t)

    for v in range(STEPS, STEPS + reach):
        advance(v)
    for k in range(reach, span + 1):
        join(k)

    ratio = vs / vp
    coef = 2.0 * ratio * ratio
    rho_vp = 2.0 * rho * vp
    rho_vs = 2.0 * rho * vs

    for half in range(halves):
        group = shot * halves + half
        level = jnp.where(group < span, span - group - 1, group - span)
        for q in range(1, na):
            pltpu.make_async_remote_copy(
                src_ref=s2.at[level], dst_ref=r2.at[na - q - 1, level],
                send_sem=r2_send.at[level], recv_sem=r2_recv.at[q - 1, level],
                device_id={"shot": mate}, device_id_type=MESH).wait_recv()

        def finish(p, carry, half=half, group=group, level=level):
            both = part[group * width + p] + r1[level, p].astype(F32)
            for q in range(1, na):
                both = both + r2[q - 1, level, p].astype(F32)
            pp = both[:width]
            ps = both[width:]
            ovp_ref[half * width + p] = rho_vp * pp
            ovs_ref[half * width + p] = rho_vs * (ps - coef * pp)
            orho_ref[half * width + p] = vp * vp * pp + vs * vs * ps
            return carry

        lax.fori_loop(0, width, finish, 0, unroll=True)

    for t in range(STEPS):
        pl.when(has_r)(lambda: halo_copy(t, True).wait_send())
        pl.when(has_l)(lambda: halo_copy(t, False).wait_send())
        for k in range(1, reach + 1):
            hop_done(t, k)
    pl.when(has_r)(lambda: rho_copy(True).wait_send())
    pl.when(has_l)(lambda: rho_copy(False).wait_send())
    for k in range(1, span + 1):
        r1_copy(k).wait_send()
        owner, q = owner_of(k)
        pl.when(owner != shot)(r2_copy(k, q, owner).wait_send)


def store(*refs):
    copies = [
        pltpu.make_async_copy(refs[i], refs[5 + i], refs[10].at[i]) for i in range(5)]
    for copy in copies:
        copy.start()
    for copy in copies:
        copy.wait()


def shards(n_slab, n_shot, source_state, receiver_state, p_velocity, s_velocity, density,
           receiver_data, source_x, source_z, receiver_x, receiver_z, offsets):
    shots, _, width, depth = source_state.shape
    noff = offsets.shape[0]
    nrec = receiver_x.shape[0]
    span = SHIFT // width
    reach = min(span, n_slab - 1)
    per = noff // n_shot
    na = n_shot // 2
    rows = 2 * shots
    slots = 2 * reach + 1
    nz = depth // LANES
    ts = STEPS * shots
    vmem = pl.BlockSpec(memory_space=pltpu.VMEM)
    hbm = pl.BlockSpec(memory_space=pltpu.HBM)
    smem = pl.BlockSpec(memory_space=pltpu.SMEM)
    image = jax.ShapeDtypeStruct((per, width, depth), F32)
    state = jax.ShapeDtypeStruct(source_state.shape, F32)
    dma = pltpu.SemaphoreType.DMA
    results = pl.pallas_call(
        functools.partial(kernel, n_slab, n_shot, reach, shots, noff),
        out_shape=(state, state, image, image, image),
        in_specs=[hbm] * 6 + [smem, smem, hbm, hbm, smem],
        out_specs=(vmem,) * 5,
        scratch_shapes=[
            pltpu.VMEM(source_state.shape, F32),
            pltpu.VMEM(source_state.shape, F32),
            pltpu.VMEM((width, depth), F32),
            pltpu.VMEM((width, depth), F32),
            pltpu.VMEM((width, depth), F32),
            pltpu.VMEM(receiver_data.shape, F32),
            pltpu.VMEM((1, nrec), jnp.int32),
            pltpu.VMEM((1, nrec), jnp.int32),
            dma((8,)),
            pltpu.VMEM((4, width, depth), F32),
            pltpu.VMEM((ts * width, depth), F32),
            pltpu.VMEM((ts * width, nrec), F32),
            pltpu.VMEM((width, depth), F32),
            pltpu.VMEM((width, depth), F32),
            pltpu.VMEM((STEPS, 4, rows, depth), F32),
            pltpu.VMEM((STEPS, 3, rows, depth), F32),
            pltpu.VMEM((STEPS, 4, rows, depth), F32),
            pltpu.VMEM((STEPS, 3, rows, depth), F32),
            pltpu.VMEM((2, rows, depth), F32),
            pltpu.VMEM((ts, nz, width, LANES), F32),
            pltpu.VMEM((STEPS, slots, shots, 2 * width, depth), BF16),
            pltpu.VMEM((2, ts, nz, (2 * span + 1) * width, LANES), F32),
            pltpu.VMEM((noff, 2 * width, depth), F32),
            pltpu.VMEM((noff, 2 * width, depth), BF16),
            pltpu.VMEM((span, width, 2 * width, depth), BF16),
            pltpu.VMEM((span, width, 2 * width, depth), BF16),
            pltpu.VMEM((na - 1, span, width, 2 * width, depth), BF16),
            dma((STEPS, 2)), dma((STEPS, 2)), dma((2,)), dma((2,)),
            dma((STEPS, slots)), dma((STEPS, slots)),
            dma((span,)), dma((span,)), dma((span,)), dma((na - 1, span)),
        ],
        compiler_params=pltpu.CompilerParams(
            collective_id=0, has_side_effects=True, vmem_limit_bytes=61 * 2**20),
    )(source_state, receiver_state, p_velocity, s_velocity, density, receiver_data,
      source_x, source_z, receiver_x.reshape(1, nrec), receiver_z.reshape(1, nrec), offsets)
    return pl.pallas_call(
        store,
        out_shape=(state, state, image, image, image),
        in_specs=[vmem] * 5,
        out_specs=(hbm,) * 5,
        scratch_shapes=[dma((5,))],
    )(*results)


def solution(mesh):
    return jax.shard_map(
        functools.partial(shards, mesh.shape["slab"], mesh.shape["shot"]),
        mesh=mesh,
        in_specs=(
            P(("group", "shot"), None, "slab", None),
            P(("group", "shot"), None, "slab", None),
            P(("group", "slab"), None),
            P(("group", "slab"), None),
            P(("group", "slab"), None),
            P(("group", "shot"), None, None),
            P(("group", "shot")),
            P(("group", "shot")),
            P("group"),
            P("group"),
            P(),
        ),
        out_specs=(
            P(("group", "shot"), None, "slab", None),
            P(("group", "shot"), None, "slab", None),
            P(("group", "shot"), "slab", None),
            P(("group", "shot"), "slab", None),
            P(("group", "shot"), "slab", None),
        ),
        check_vma=False,
    )
```
